32 devices in a mesh: groups: 2 (over x), attn: 2 (over core), expert: 8 (over z, y).
Axes of the slice: x: 2, y: 2, z: 4, core: 2. Of those that a mesh axis runs over, the one named last changes fastest.
Arguments:
- hidden_a: bfloat16 [1024, 1440], P(('groups', 'attn', 'expert')), parts along dimension 0, may hold values from -6 to 6
- routes: int32 [1024, 4], P(('groups', 'attn', 'expert')), parts along dimension 0, may hold values from 0 to 15, all different within a row; in each aligned block of 32 rows (0 to 31, 32 to 63, ...) at most 16 rows name the same one
- gate_w: bfloat16 [1024, 4], P(('groups', 'attn', 'expert')), parts along dimension 0, may hold values from 0.049804688 to 0.59765625
- w_gate: bfloat16 [16, 1440, 1440], P(('attn', 'expert')), may hold values from -0.15625 to 0.15625
- w_up: bfloat16 [16, 1440, 1440], P(('attn', 'expert')), may hold values from -0.15625 to 0.15625
- w_down: bfloat16 [16, 1440, 1440], P(('attn', 'expert')), may hold values from -0.15625 to 0.15625
Outputs:
- mixed: bfloat16 [1024, 1440], P(('groups', 'attn', 'expert')), parts along dimension 0
The draws below stay inside these ranges and needn't reach their ends.
There are 2 independent parts, one for each index of `groups`. The reference program is written for one: setup_inputs(seed, part) draws one part's arguments, and reference() takes and returns one part's arrays. A program takes and returns all parts, laid end to end along the dimension named above; an argument that names none is the same for every part. Nothing has to cross between parts.
Inputs may be any that keep to these rules, and one draw needn't show every extreme that they name: `routes`: in the rows of one device, each expert is named by at most 16 rows; a token names 4 different experts.
All inputs are finite; a program needn't handle non-finite values.
Results may differ from the reference program's by a relative error of at most 0.0058.
Values may be sent and summed in bfloat16 or wider, within the bound.
A program may use at most 64 MiB of HBM per device.

```python
import math
import jax
import jax.numpy as jnp
import numpy as np
from jax import lax

D = 1440
FF = 1440
TOP = 4
TOK_DEV = 32
EXPERTS = 16
CAP = 16
TOKENS = 512


def block_levels(stream_key, extent, cuts, low, high):
    gain = 1.0
    for axis_at, blocks in cuts:
        draws = jax.random.uniform(jax.random.fold_in(jax.random.fold_in(stream_key, 6), axis_at), (blocks,), jnp.float32, low / len(cuts), high / len(cuts))
        gain = gain * jnp.repeat(jnp.exp(draws), extent[axis_at] // blocks).reshape((-1,) + (1,) * (len(extent) - 1 - axis_at))
    return gain


def routed_block(own_key, own, number, rows, amount, top, bound, lean):
    order = jax.random.permutation(own_key, amount)
    crowded, common = load_shares(amount, rows * top, bound, lean, True), load_shares(amount, rows * top, bound, lean, False)
    places = jnp.arange(amount)

    def named(tallies, rotation):
        used = int((tallies > 0).sum())
        fixed = max(1, used // 4)
        shifted = fixed + (places - fixed + rotation * (used - fixed)) % max(1, amount - fixed)
        return jnp.zeros((amount,), jnp.int32).at[order[jnp.where(places < fixed, places, shifted)]].set(jnp.asarray(tallies, jnp.int32))

    tallies = jnp.where(number % 4 == 0, named(crowded, number // 4), named(common, number - number // 4 - 1))
    mixed = jax.random.permutation(jax.random.fold_in(own, 3), amount)
    source_of, sink = mixed[0:amount // 2 * 2:2], mixed[1:amount // 2 * 2:2]
    slack = jnp.minimum(tallies[source_of] - 1, bound - tallies[sink]) // 2
    slack = jnp.where((source_of == order[0]) | (sink == order[0]) | (tallies[sink] == 0), 0, jnp.maximum(slack, 0))
    shifted = jax.random.randint(jax.random.fold_in(own, 4), (amount // 2,), 0, 1 << 20) % (slack + 1)
    tallies = tallies.at[source_of].add(-shifted).at[sink].add(shifted)
    members = jnp.searchsorted(jnp.cumsum(tallies), jnp.arange(rows * top), side="right").astype(jnp.int32)
    table = members.reshape(top, rows).T
    table = table[jax.random.permutation(jax.random.fold_in(own, 1), rows)]
    rotation = jax.random.randint(jax.random.fold_in(own, 2), (rows, 1), 0, top)
    return jnp.take_along_axis(table, (jnp.arange(top)[None, :] + rotation) % top, axis=1)


def load_shares(count, total, reach, slope, full):
    loads = [(1 << 20) // math.isqrt(rank ** slope) + 1 for rank in range(1, count + 1)]
    largest = reach if full else min(reach, max(-(-total // count), total * loads[0] // sum(loads)))
    least = 1 if total - largest >= count - 1 else 0
    given, spare = [largest] + [least] * (count - 1), total - largest - least * (count - 1)
    while spare > 0:
        movable = [i for i in range(1, count) if given[i] < largest] or [i for i in range(1, count) if given[i] < reach]
        mass, budget = sum([loads[i] for i in movable]), spare
        for i in movable:
            more = min(reach - given[i], max(1, budget * loads[i] // mass), spare)
            given[i] = given[i] + more
            spare = spare - more
    return np.array(given)


def normal_values(rng, extent, spread, reach, shards=(), kind=jnp.bfloat16):
    gain = block_levels(rng, extent, shards, -0.22, 0.18) if shards else 1.0
    drawn = jax.random.normal(rng, extent, jnp.float32) * spread * gain
    return jnp.minimum(jnp.maximum(drawn, -reach), reach).astype(kind)


def setup_inputs(seed: int = 0, part: int = 0) -> dict:
    keys = jax.random.split(jax.random.key(seed), 7)
    part_keys = jax.random.split(jax.random.fold_in(keys[6], part), 7)
    hidden_a = normal_values(part_keys[0], (TOKENS, D), 1.0, 6.0, ((0, 16),))
    routes_keys = jax.random.split(jax.random.fold_in(part_keys[1], 1), TOKENS // TOK_DEV)
    routes_turns = jax.random.permutation(jax.random.fold_in(part_keys[1], 3), TOKENS // TOK_DEV)
    routes = jax.vmap(lambda own, number: routed_block(jax.random.fold_in(part_keys[1], 2), own, number, TOK_DEV, EXPERTS, TOP, CAP, 2))(routes_keys, routes_turns).reshape((TOKENS, TOP))
    gate_w = jnp.clip(0.049804688 + 0.54785156 * jax.random.uniform(part_keys[2], (TOKENS, TOP), jnp.float32) ** block_levels(part_keys[2], (TOKENS, TOP), ((0, 16),), -0.2, 0.2), 0.049804688, 0.59765625).astype(jnp.bfloat16)
    w_gate = normal_values(keys[3], (EXPERTS, D, FF), D ** -0.5, 0.15625, ((0, 16),))
    w_up = normal_values(keys[4], (EXPERTS, D, FF), D ** -0.5, 0.15625, ((0, 16),))
    w_down = normal_values(keys[5], (EXPERTS, FF, D), FF ** -0.5, 0.15625, ((0, 16),))
    return dict(hidden_a=hidden_a, routes=routes, gate_w=gate_w, w_gate=w_gate, w_up=w_up, w_down=w_down)


def slots_of(block_routes):
    flat = block_routes.reshape(-1)
    hits = (flat[:, None] == jnp.arange(EXPERTS, dtype=jnp.int32)[None, :]).astype(jnp.int32)
    before = jnp.cumsum(hits, axis=0) - hits
    rank = jnp.sum(before * hits, axis=1).astype(jnp.int32)
    return (flat * CAP + rank).astype(jnp.int32)


def fill_table(position):
    empty = jnp.full((EXPERTS * CAP,), -1, dtype=jnp.int32)
    return empty.at[position].set(jnp.arange(TOK_DEV * TOP, dtype=jnp.int32))


def reference(hidden_a, routes, gate_w, w_gate, w_up, w_down):
    blocks = TOKENS // TOK_DEV
    positions = jax.vmap(slots_of)(routes.reshape(blocks, TOK_DEV, TOP))
    table = jax.vmap(fill_table)(positions).reshape(blocks, EXPERTS, CAP).transpose(1, 0, 2)
    block_base = (jnp.arange(blocks, dtype=jnp.int32) * TOK_DEV)[:, None]
    flat_weights = gate_w.reshape(-1)

    def one_expert(index):
        ids = table[index]
        live = ids >= 0
        safe = jnp.maximum(ids, 0)
        token = (block_base + safe // TOP).astype(jnp.int32)
        rows = jnp.where(live[..., None], hidden_a[token], jnp.zeros((), jnp.bfloat16)).reshape(-1, D)
        weights = jnp.where(live, flat_weights[(block_base * TOP + safe).astype(jnp.int32)], jnp.zeros((), jnp.bfloat16))
        rows_f = rows.astype(jnp.float32)
        gate = jnp.dot(rows_f, w_gate[index].astype(jnp.float32))
        up = jnp.dot(rows_f, w_up[index].astype(jnp.float32))
        hidden = lax.optimization_barrier((jax.nn.silu(gate) * up).astype(jnp.bfloat16))
        down = jnp.dot(hidden.astype(jnp.float32), w_down[index].astype(jnp.float32))
        result = (weights.reshape(-1, 1).astype(jnp.float32) * down).astype(jnp.bfloat16)
        return result.reshape(blocks, CAP, D)

    results = lax.map(one_expert, jnp.arange(EXPERTS, dtype=jnp.int32))
    expert_of = positions // CAP
    slot_of = positions % CAP
    block_of = jnp.broadcast_to(jnp.arange(blocks, dtype=jnp.int32)[:, None], positions.shape)
    taken = results[expert_of, block_of, slot_of]
    mixed = jnp.sum(taken.astype(jnp.float32).reshape(TOKENS, TOP, D), axis=1).astype(jnp.bfloat16)
    return mixed
```

```python
import functools
import jax
import jax.numpy as jnp
from jax import lax
from jax.experimental import pallas as pl
from jax.experimental.pallas import tpu as pltpu
from jax.sharding import PartitionSpec as P

MESH = pl.DeviceIdType.MESH
FAR = 4
LANES = 128


def exchange_body(hidden_a, routes, gate_w, w_gate, w_up, w_down):
    experts = lax.axis_size(("attn", "expert"))
    tok_dev, top_k = routes.shape
    width = hidden_a.shape[1]
    capacity = 2 * tok_dev * top_k // experts
    flat = routes.reshape(-1)
    hits = (flat[:, None] == jnp.arange(experts, dtype=jnp.int32)[None, :]).astype(jnp.int32)
    rank = jnp.sum((jnp.cumsum(hits, axis=0) - hits) * hits, axis=1)
    position = flat * capacity + rank
    source = (
        jnp.full((experts * capacity,), -1, dtype=jnp.int32)
        .at[position]
        .set(jnp.arange(tok_dev * top_k, dtype=jnp.int32))
    )
    live = source >= 0
    safe = jnp.maximum(source, 0)
    send_rows = jnp.where(live[:, None], hidden_a[safe // top_k], jnp.zeros((), jnp.bfloat16))
    send_rows = send_rows.reshape(experts, capacity, width)
    send_weights = jnp.where(live, gate_w.reshape(-1)[safe], jnp.zeros((), jnp.bfloat16))
    send_weights = send_weights.reshape(experts, capacity)
    weights = lax.all_to_all(
        send_weights, ("attn", "expert"), split_axis=0, concat_axis=0, tiled=True
    )
    senders, slots = weights.shape
    flat_rows = lax.all_to_all(
        send_rows, ("attn", "expert"), split_axis=0, concat_axis=0, tiled=True
    ).reshape(senders * slots, width)
    gate = jnp.dot(flat_rows, w_gate[0], preferred_element_type=jnp.float32)
    up = jnp.dot(flat_rows, w_up[0], preferred_element_type=jnp.float32)
    hidden = (jax.nn.silu(gate) * up).astype(jnp.bfloat16)
    down = jnp.dot(hidden, w_down[0], preferred_element_type=jnp.float32)
    scaled = weights.reshape(-1, 1).astype(jnp.float32) * down
    produced = scaled.astype(jnp.bfloat16).reshape(senders, slots, width)
    returned = lax.all_to_all(produced, ("attn", "expert"), split_axis=0, concat_axis=0, tiled=True)
    results = returned.reshape(experts * capacity, width)
    taken = results[position]
    return jnp.sum(taken.astype(jnp.float32).reshape(tok_dev, top_k, width), axis=1).astype(
        jnp.bfloat16
    )


def tiles_of(total, step):
    return [(at, min(step, total - at)) for at in range(0, total, step)]


def kernel(
    hidden_ref, routes_ref, gates_ref, wg_hbm, wu_hbm, wd_hbm, out_ref,
    wg, wu, wd, x, h, y, from_core, to_y, from_y, to_z, from_z,
    load_sem, ag_send, ag_recv, core_send, core_recv, y_send, y_recv, z_send, z_recv,
):
    rows, top = routes_ref.shape
    width = hidden_ref.shape[1]
    ff = wg_hbm.shape[2]
    quad = FAR * rows

    group = lax.axis_index("groups")
    core = lax.axis_index("attn")
    place = lax.axis_index("expert")
    far, near = place // 2, place % 2
    own = core * lax.axis_size("expert") + place

    fars = [far, far + 1 - 2 * (far % 2), (far + 2) % FAR, FAR - 1 - far]
    sibling = (group, 1 - core, place)
    beside = (group, core, far * 2 + 1 - near)
    along = [(group, core, f * 2 + near) for f in fars]

    loads = [
        pltpu.make_async_copy(src.at[0], dst, load_sem.at[i])
        for i, (src, dst) in enumerate(((wg_hbm, wg), (wu_hbm, wu), (wd_hbm, wd)))
    ]
    for load in loads:
        load.start()

    barrier = pltpu.get_barrier_semaphore()
    partners = [sibling, beside] + along[1:]
    for partner in partners:
        pl.semaphore_signal(barrier, inc=1, device_id=partner, device_id_type=MESH)

    start = width // LANES * LANES
    rest = width - start
    x[0:rows, 0:start] = hidden_ref[:, 0:start]
    lane = lax.broadcasted_iota(jnp.int32, (rows, LANES), 1)
    table = jnp.zeros((rows, LANES), jnp.float32)
    for k in range(top):
        table += jnp.where(
            lane == routes_ref[:, k : k + 1] + rest, gates_ref[:, k : k + 1].astype(jnp.float32), 0.0
        )
    last = jnp.concatenate(
        [hidden_ref[:, start:].astype(jnp.float32), jnp.zeros((rows, LANES - rest), jnp.float32)], axis=1
    )
    x[0:rows, start : start + LANES] = (table + last).astype(jnp.bfloat16)
    pl.semaphore_wait(barrier, len(partners))

    def slot(dy, dc, d):
        return x.at[pl.ds(((dy * 2 + dc) * FAR + d) * rows, rows)]

    def remote(src, dst, send, recv, i, device):
        return pltpu.make_async_remote_copy(
            src_ref=src, dst_ref=dst, send_sem=send.at[i], recv_sem=recv.at[i],
            device_id=device, device_id_type=MESH,
        )

    gather_z = {d: remote(slot(0, 0, 0), slot(0, 0, d), ag_send, ag_recv, d - 1, along[d]) for d in (1, 2, 3)}
    gather_y = {d: remote(slot(0, 0, d), slot(1, 0, d), ag_send, ag_recv, 3 + d, beside) for d in range(FAR)}
    gather_c = {
        (dy, d): remote(slot(dy, 0, d), slot(dy, 1, d), ag_send, ag_recv, 7 + dy * FAR + d, sibling)
        for dy in range(2) for d in range(FAR)
    }
    for d in (3, 2, 1):
        gather_z[d].start()
    gather_y[0].start()
    gather_c[0, 0].start()
    for d in (1, 2, 3):
        gather_z[d].wait_recv()
        gather_y[d].start()
        gather_c[0, d].start()

    n_ff = tiles_of(ff, 512)
    n_out = tiles_of(width, 512)
    scale = {}

    def up_tile(dy, at, size):
        block = x[dy * 2 * quad : (dy + 1) * 2 * quad, 0:width]
        gate = jnp.dot(block, wg[:, at : at + size], preferred_element_type=jnp.float32)
        up = jnp.dot(block, wu[:, at : at + size], preferred_element_type=jnp.float32)
        h[:, at : at + size] = (gate / (1.0 + jnp.exp(-gate)) * up).astype(jnp.bfloat16)

    def down_tile(dy, at, size):
        if dy not in scale:
            tail = x[dy * 2 * quad : (dy + 1) * 2 * quad, start : start + LANES].astype(jnp.float32)
            lanes = lax.broadcasted_iota(jnp.int32, tail.shape, 1)
            scale[dy] = jnp.sum(jnp.where(lanes == own + rest, tail, 0.0), axis=1, keepdims=True)
        down = jnp.dot(h[...], wd[:, at : at + size], preferred_element_type=jnp.float32)
        y[dy * 2 * quad : (dy + 1) * 2 * quad, at : at + size] = (scale[dy] * down).astype(jnp.bfloat16)

    def core_copy(dy, j):
        at, size = n_out[j]
        columns = pl.ds(at, size)
        return remote(
            y.at[pl.ds((dy * 2 + 1) * quad, quad), columns],
            from_core.at[pl.ds(dy * quad, quad), columns],
            core_send, core_recv, dy * len(n_out) + j, sibling,
        )

    def y_copy(j):
        columns = pl.ds(*n_out[j])
        return remote(to_y.at[:, columns], from_y.at[:, columns], y_send, y_recv, j, beside)

    def z_copy(j, d):
        columns = pl.ds(*n_out[j])
        return remote(
            to_z.at[pl.ds(d * rows, rows), columns], from_z.at[pl.ds(d * rows, rows), columns],
            z_send, z_recv, j * 3 + d - 1, along[d],
        )

    for d in range(FAR):
        gather_c[0, d].wait_recv()
    loads[0].wait()
    loads[1].wait()
    for at, size in n_ff:
        up_tile(0, at, size)
    for d in range(FAR):
        gather_y[d].wait_recv()
        gather_c[1, d].start()
    loads[2].wait()
    for j, (at, size) in enumerate(n_out):
        down_tile(0, at, size)
        core_copy(0, j).start()

    for d in range(FAR):
        gather_c[1, d].wait_recv()
    for at, size in n_ff:
        up_tile(1, at, size)

    def after_core(j):
        at, size = n_out[j]
        core_copy(1, j).wait_recv()
        to_y[:, at : at + size] = (
            y[2 * quad : 3 * quad, at : at + size].astype(jnp.float32)
            + from_core[quad : 2 * quad, at : at + size].astype(jnp.float32)
        ).astype(jnp.bfloat16)
        y_copy(j).start()

    def after_y(j):
        at, size = n_out[j]
        core_copy(0, j).wait_recv()
        y_copy(j).wait_recv()
        to_z[:, at : at + size] = (
            y[0:quad, at : at + size].astype(jnp.float32)
            + from_core[0:quad, at : at + size].astype(jnp.float32)
            + from_y[:, at : at + size].astype(jnp.float32)
        ).astype(jnp.bfloat16)
        for d in (3, 2, 1):
            z_copy(j, d).start()

    count = len(n_out)
    for j, (at, size) in enumerate(n_out):
        down_tile(1, at, size)
        core_copy(1, j).start()
        if j >= 1:
            after_core(j - 1)
    after_core(count - 1)
    for j in range(count):
        after_y(j)
    for j, (at, size) in enumerate(n_out):
        total = to_z[0:rows, at : at + size].astype(jnp.float32)
        for d in (1, 2, 3):
            z_copy(j, d).wait_recv()
            total += from_z[d * rows : (d + 1) * rows, at : at + size].astype(jnp.float32)
        out_ref[:, at : at + size] = total.astype(jnp.bfloat16)

    for copy in [*gather_z.values(), *gather_y.values(), *gather_c.values()]:
        copy.wait_send()
    for j in range(count):
        core_copy(0, j).wait_send()
        core_copy(1, j).wait_send()
        y_copy(j).wait_send()
        for d in (1, 2, 3):
            z_copy(j, d).wait_send()


def gather_body(hidden_a, routes, gate_w, w_gate, w_up, w_down):
    experts = lax.axis_size(("attn", "expert"))
    rows, width = hidden_a.shape
    ff = w_gate.shape[2]
    wide = -(-width // LANES) * LANES
    quad = FAR * rows
    count = len(tiles_of(width, 512))
    vmem = pl.BlockSpec(memory_space=pltpu.VMEM)
    hbm = pl.BlockSpec(memory_space=pl.ANY)
    dma = pltpu.SemaphoreType.DMA
    tokens = experts * rows
    return pl.pallas_call(
        kernel,
        out_shape=jax.ShapeDtypeStruct((rows, width), jnp.bfloat16),
        in_specs=[vmem, vmem, vmem, hbm, hbm, hbm],
        out_specs=vmem,
        scratch_shapes=[
            pltpu.VMEM((width, ff), jnp.bfloat16),
            pltpu.VMEM((width, ff), jnp.bfloat16),
            pltpu.VMEM((ff, width), jnp.bfloat16),
            pltpu.VMEM((tokens, wide), jnp.bfloat16),
            pltpu.VMEM((tokens // 2, ff), jnp.bfloat16),
            pltpu.VMEM((tokens, width), jnp.bfloat16),
            pltpu.VMEM((tokens // 2, width), jnp.bfloat16),
            pltpu.VMEM((quad, width), jnp.bfloat16),
            pltpu.VMEM((quad, width), jnp.bfloat16),
            pltpu.VMEM((quad, width), jnp.bfloat16),
            pltpu.VMEM((quad, width), jnp.bfloat16),
            dma((3,)),
            dma((15,)),
            dma((15,)),
            dma((2 * count,)),
            dma((2 * count,)),
            dma((count,)),
            dma((count,)),
            dma((3 * count,)),
            dma((3 * count,)),
        ],
        compiler_params=pltpu.CompilerParams(
            collective_id=0, has_side_effects=True, vmem_limit_bytes=56 * 1024 * 1024
        ),
        cost_estimate=pl.CostEstimate(
            flops=6 * tokens * width * ff, bytes_accessed=6 * width * ff, transcendentals=tokens * ff
        ),
    )(hidden_a, routes, gate_w, w_gate, w_up, w_down)


def solution(mesh):
    placed = (
        P(("groups", "attn", "expert"), None),
        P(("groups", "attn", "expert"), None),
        P(("groups", "attn", "expert"), None),
        P(("attn", "expert"), None, None),
        P(("attn", "expert"), None, None),
        P(("attn", "expert"), None, None),
    )
    small = mesh.shape["attn"] == 2 and mesh.shape["expert"] == 2 * FAR
    return jax.shard_map(
        gather_body if small else exchange_body,
        mesh=mesh,
        in_specs=placed,
        out_specs=P(("groups", "attn", "expert"), None),
        check_vma=False,
    )
```

```python
import functools
import jax
import jax.numpy as jnp
from jax import lax
from jax.experimental import pallas as pl
from jax.experimental.pallas import tpu as pltpu
from jax.sharding import PartitionSpec as P

MESH = pl.DeviceIdType.MESH
FAR = 4
LANES = 128


def exchange_body(hidden_a, routes, gate_w, w_gate, w_up, w_down):
    experts = lax.axis_size(("attn", "expert"))
    tok_dev, top_k = routes.shape
    width = hidden_a.shape[1]
    capacity = 2 * tok_dev * top_k // experts
    flat = routes.reshape(-1)
    hits = (flat[:, None] == jnp.arange(experts, dtype=jnp.int32)[None, :]).astype(jnp.int32)
    rank = jnp.sum((jnp.cumsum(hits, axis=0) - hits) * hits, axis=1)
    position = flat * capacity + rank
    source = (
        jnp.full((experts * capacity,), -1, dtype=jnp.int32)
        .at[position]
        .set(jnp.arange(tok_dev * top_k, dtype=jnp.int32))
    )
    live = source >= 0
    safe = jnp.maximum(source, 0)
    send_rows = jnp.where(live[:, None], hidden_a[safe // top_k], jnp.zeros((), jnp.bfloat16))
    send_rows = send_rows.reshape(experts, capacity, width)
    send_weights = jnp.where(live, gate_w.reshape(-1)[safe], jnp.zeros((), jnp.bfloat16))
    send_weights = send_weights.reshape(experts, capacity)
    weights = lax.all_to_all(
        send_weights, ("attn", "expert"), split_axis=0, concat_axis=0, tiled=True
    )
    senders, slots = weights.shape
    flat_rows = lax.all_to_all(
        send_rows, ("attn", "expert"), split_axis=0, concat_axis=0, tiled=True
    ).reshape(senders * slots, width)
    gate = jnp.dot(flat_rows, w_gate[0], preferred_element_type=jnp.float32)
    up = jnp.dot(flat_rows, w_up[0], preferred_element_type=jnp.float32)
    hidden = (jax.nn.silu(gate) * up).astype(jnp.bfloat16)
    down = jnp.dot(hidden, w_down[0], preferred_element_type=jnp.float32)
    scaled = weights.reshape(-1, 1).astype(jnp.float32) * down
    produced = scaled.astype(jnp.bfloat16).reshape(senders, slots, width)
    returned = lax.all_to_all(produced, ("attn", "expert"), split_axis=0, concat_axis=0, tiled=True)
    results = returned.reshape(experts * capacity, width)
    taken = results[position]
    return jnp.sum(taken.astype(jnp.float32).reshape(tok_dev, top_k, width), axis=1).astype(
        jnp.bfloat16
    )


def tiles_of(total, step):
    return [(at, min(step, total - at)) for at in range(0, total, step)]


def kernel(
    hidden_hbm, routes_hbm, gates_hbm, wg_hbm, wu_hbm, wd_hbm, out_ref,
    tokens, named, gates, wg, wu, wd, x, h, y, from_core, to_y, from_y, to_z, from_z,
    load_sem, ag_send, ag_recv, core_send, core_recv, y_send, y_recv, z_send, z_recv,
):
    top, rows = routes_hbm.shape
    width = hidden_hbm.shape[1]
    ff = wg_hbm.shape[2]
    quad = FAR * rows

    group = lax.axis_index("groups")
    core = lax.axis_index("attn")
    place = lax.axis_index("expert")
    far, near = place // 2, place % 2
    own = core * lax.axis_size("expert") + place

    fars = [far, far + 1 - 2 * (far % 2), (far + 2) % FAR, FAR - 1 - far]
    sibling = (group, 1 - core, place)
    beside = (group, core, far * 2 + 1 - near)
    along = [(group, core, f * 2 + near) for f in fars]

    inputs = [
        pltpu.make_async_copy(src, dst, load_sem.at[i])
        for i, (src, dst) in enumerate(((hidden_hbm, tokens), (routes_hbm, named), (gates_hbm, gates)))
    ]
    loads = [
        pltpu.make_async_copy(src.at[0], dst, load_sem.at[3 + i])
        for i, (src, dst) in enumerate(((wg_hbm, wg), (wu_hbm, wu), (wd_hbm, wd)))
    ]
    for load in inputs:
        load.start()

    barrier = pltpu.get_barrier_semaphore()
    partners = [sibling, beside] + along[1:]
    for partner in partners:
        pl.semaphore_signal(barrier, inc=1, device_id=partner, device_id_type=MESH)

    for load in loads:
        load.start()
    for load in inputs:
        load.wait()

    start = width // LANES * LANES
    rest = width - start
    x[0:rows, 0:start] = tokens[:, 0:start]
    lane = lax.broadcasted_iota(jnp.int32, (LANES, rows), 0)
    weights = gates[...].astype(jnp.float32)
    table = jnp.zeros((LANES, rows), jnp.float32)
    for k in range(top):
        table += jnp.where(lane == named[k : k + 1, :] + rest, weights[k : k + 1, :], 0.0)
    last = jnp.concatenate(
        [tokens[:, start:].astype(jnp.float32), jnp.zeros((rows, LANES - rest), jnp.float32)], axis=1
    )
    x[0:rows, start : start + LANES] = (table.T + last).astype(jnp.bfloat16)
    pl.semaphore_wait(barrier, len(partners))

    half = rows // 2

    def piece(dy, dc, d, p):
        return x.at[pl.ds(((dy * 2 + dc) * FAR + d) * rows + p * half, half)]

    def remote(src, dst, send, recv, device):
        return pltpu.make_async_remote_copy(
            src_ref=src, dst_ref=dst, send_sem=send, recv_sem=recv,
            device_id=device, device_id_type=MESH,
        )

    def gather(src, dst, i, device):
        return remote(src, dst, ag_send.at[i], ag_recv.at[i], device)

    middle = (far + 1) // 2 == 1
    pieces = range(2)
    gather_z = {
        (d, p): gather(piece(0, 0, 0, p), piece(0, 0, d, p), (d - 1) * 2 + p, along[d])
        for d in (1, 2, 3) for p in pieces
    }
    gather_y = {
        (d, p): gather(piece(0, 0, d, p), piece(1, 0, d, p), 6 + d * 2 + p, beside)
        for d in range(FAR) for p in pieces
    }
    gather_c = {
        (dy, d, p): gather(piece(dy, 0, d, p), piece(dy, 1, d, p), 14 + (dy * FAR + d) * 2 + p, sibling)
        for dy in range(2) for d in range(FAR) for p in pieces
    }
    passed = {
        p: remote(piece(0, 0, 2, p), piece(0, 0, 3, p), ag_send.at[30 + p], ag_recv.at[4 + p], along[1])
        for p in pieces
    }
    for p in pieces:
        gather_z[2, p].start()
        gather_z[1, p].start()
        gather_y[0, p].start()

    @pl.when(middle)
    def _():
        for p in pieces:
            gather_z[3, p].start()

    for p in pieces:
        gather_c[0, 0, p].start()
    for d, p in ((2, 0), (1, 0), (2, 1), (1, 1), (3, 0), (3, 1)):
        gather_z[d, p].wait_recv()
        if d == 2:

            @pl.when(middle)
            def _():
                passed[p].start()

        gather_y[d, p].start()
        gather_c[0, d, p].start()

    n_ff = tiles_of(ff, 512)
    n_out = tiles_of(width, 256)
    scale = {}

    def up_tile(dy, at, size):
        block = x[dy * 2 * quad : (dy + 1) * 2 * quad, 0:width]
        gate = jnp.dot(block, wg[:, at : at + size], preferred_element_type=jnp.float32)
        up = jnp.dot(block, wu[:, at : at + size], preferred_element_type=jnp.float32)
        h[:, at : at + size] = (gate / (1.0 + jnp.exp(-gate)) * up).astype(jnp.bfloat16)

    def down_tile(dy, at, size):
        if dy not in scale:
            tail = x[dy * 2 * quad : (dy + 1) * 2 * quad, start : start + LANES].astype(jnp.float32)
            lanes = lax.broadcasted_iota(jnp.int32, tail.shape, 1)
            scale[dy] = jnp.sum(jnp.where(lanes == own + rest, tail, 0.0), axis=1, keepdims=True)
        down = jnp.dot(h[...], wd[:, at : at + size], preferred_element_type=jnp.float32)
        y[dy * 2 * quad : (dy + 1) * 2 * quad, at : at + size] = (scale[dy] * down).astype(jnp.bfloat16)

    early = remote(
        y.at[pl.ds(quad, quad)], from_core.at[pl.ds(0, quad)], core_send.at[0], core_recv.at[0], sibling
    )

    def core_copy(j):
        columns = pl.ds(*n_out[j])
        return remote(
            y.at[pl.ds(3 * quad, quad), columns],
            from_core.at[pl.ds(quad, quad), columns],
            core_send.at[1 + j], core_recv.at[1 + j], sibling,
        )

    def y_copy(j):
        columns = pl.ds(*n_out[j])
        return remote(to_y.at[:, columns], from_y.at[:, columns], y_send.at[j], y_recv.at[j], beside)

    def z_copy(j, d):
        columns = pl.ds(*n_out[j])
        i = j * 3 + d - 1
        return remote(
            to_z.at[pl.ds(d * rows, rows), columns], from_z.at[pl.ds(d * rows, rows), columns],
            z_send.at[i], z_recv.at[i], along[d],
        )

    for d in range(FAR):
        for p in pieces:
            gather_c[0, d, p].wait_recv()
    loads[0].wait()
    loads[1].wait()
    for at, size in n_ff:
        up_tile(0, at, size)
    queue = [(0, 0), (0, 1), (2, 0), (1, 0), (2, 1), (1, 1), (3, 0), (3, 1)]

    def hand_on(many):
        for _ in range(many):
            d, p = queue.pop(0)
            gather_y[d, p].wait_recv()
            gather_c[1, d, p].start()

    hand_on(4)
    loads[2].wait()
    for j, (at, size) in enumerate(n_out):
        down_tile(0, at, size)
        if j >= 1 and len(queue) > 0:
            hand_on(1)
    hand_on(len(queue))
    early.start()

    for d in range(FAR):
        for p in pieces:
            gather_c[1, d, p].wait_recv()
    for at, size in n_ff:
        up_tile(1, at, size)

    def after_core(j):
        at, size = n_out[j]
        core_copy(j).wait_recv()
        to_y[:, at : at + size] = (
            y[2 * quad : 3 * quad, at : at + size].astype(jnp.float32)
            + from_core[quad : 2 * quad, at : at + size].astype(jnp.float32)
        ).astype(jnp.bfloat16)
        y_copy(j).start()

    def after_y(j):
        at, size = n_out[j]
        y_copy(j).wait_recv()
        to_z[:, at : at + size] = (
            y[0:quad, at : at + size].astype(jnp.float32)
            + from_core[0:quad, at : at + size].astype(jnp.float32)
            + from_y[:, at : at + size].astype(jnp.float32)
        ).astype(jnp.bfloat16)
        for d in (3, 2, 1):
            z_copy(j, d).start()

    count = len(n_out)
    for j, (at, size) in enumerate(n_out):
        down_tile(1, at, size)
        core_copy(j).start()
        if j >= 1:
            after_core(j - 1)
    after_core(count - 1)
    early.wait_recv()
    for j in range(count):
        after_y(j)
    for j, (at, size) in enumerate(n_out):
        total = to_z[0:rows, at : at + size].astype(jnp.float32)
        for d in (1, 2, 3):
            z_copy(j, d).wait_recv()
            total += from_z[d * rows : (d + 1) * rows, at : at + size].astype(jnp.float32)
        out_ref[:, at : at + size] = total.astype(jnp.bfloat16)

    for d in (1, 2):
        for p in pieces:
            gather_z[d, p].wait_send()

    @pl.when(middle)
    def _():
        for p in pieces:
            gather_z[3, p].wait_send()
            passed[p].wait_send()

    for copy in [*gather_y.values(), *gather_c.values()]:
        copy.wait_send()
    early.wait_send()
    for j in range(count):
        core_copy(j).wait_send()
        y_copy(j).wait_send()
        for d in (1, 2, 3):
            z_copy(j, d).wait_send()


def gather_body(hidden_a, routes, gate_w, w_gate, w_up, w_down):
    experts = lax.axis_size(("attn", "expert"))
    rows, width = hidden_a.shape
    ff = w_gate.shape[2]
    wide = -(-width // LANES) * LANES
    quad = FAR * rows
    count = len(tiles_of(width, 256))
    vmem = pl.BlockSpec(memory_space=pltpu.VMEM)
    hbm = pl.BlockSpec(memory_space=pl.ANY)
    dma = pltpu.SemaphoreType.DMA
    tokens = experts * rows
    return pl.pallas_call(
        kernel,
        out_shape=jax.ShapeDtypeStruct((rows, width), jnp.bfloat16),
        in_specs=[hbm] * 6,
        out_specs=vmem,
        scratch_shapes=[
            pltpu.VMEM((rows, width), jnp.bfloat16),
            pltpu.VMEM(routes.shape[::-1], jnp.int32),
            pltpu.VMEM(gate_w.shape[::-1], jnp.bfloat16),
            pltpu.VMEM((width, ff), jnp.bfloat16),
            pltpu.VMEM((width, ff), jnp.bfloat16),
            pltpu.VMEM((ff, width), jnp.bfloat16),
            pltpu.VMEM((tokens, wide), jnp.bfloat16),
            pltpu.VMEM((tokens // 2, ff), jnp.bfloat16),
            pltpu.VMEM((tokens, width), jnp.bfloat16),
            pltpu.VMEM((tokens // 2, width), jnp.bfloat16),
            pltpu.VMEM((quad, width), jnp.bfloat16),
            pltpu.VMEM((quad, width), jnp.bfloat16),
            pltpu.VMEM((quad, width), jnp.bfloat16),
            pltpu.VMEM((quad, width), jnp.bfloat16),
            dma((6,)),
            dma((32,)),
            dma((30,)),
            dma((1 + count,)),
            dma((1 + count,)),
            dma((count,)),
            dma((count,)),
            dma((3 * count,)),
            dma((3 * count,)),
        ],
        compiler_params=pltpu.CompilerParams(
            collective_id=0, has_side_effects=True, vmem_limit_bytes=56 * 1024 * 1024
        ),
        cost_estimate=pl.CostEstimate(
            flops=6 * tokens * width * ff, bytes_accessed=6 * width * ff, transcendentals=tokens * ff
        ),
    )(hidden_a, routes.T, gate_w.T, w_gate, w_up, w_down)


def solution(mesh):
    placed = (
        P(("groups", "attn", "expert"), None),
        P(("groups", "attn", "expert"), None),
        P(("groups", "attn", "expert"), None),
        P(("attn", "expert"), None, None),
        P(("attn", "expert"), None, None),
        P(("attn", "expert"), None, None),
    )
    small = mesh.shape["attn"] == 2 and mesh.shape["expert"] == 2 * FAR
    return jax.shard_map(
        gather_body if small else exchange_body,
        mesh=mesh,
        in_specs=placed,
        out_specs=P(("groups", "attn", "expert"), None),
        check_vma=False,
    )
```

```python
import functools
import jax
import jax.numpy as jnp
from jax import lax
from jax.experimental import pallas as pl
from jax.experimental.pallas import tpu as pltpu
from jax.sharding import PartitionSpec as P

MESH = pl.DeviceIdType.MESH
FAR = 4
LANES = 128


def exchange_body(hidden_a, routes, gate_w, w_gate, w_up, w_down):
    experts = lax.axis_size(("attn", "expert"))
    tok_dev, top_k = routes.shape
    width = hidden_a.shape[1]
    capacity = 2 * tok_dev * top_k // experts
    flat = routes.reshape(-1)
    hits = (flat[:, None] == jnp.arange(experts, dtype=jnp.int32)[None, :]).astype(jnp.int32)
    rank = jnp.sum((jnp.cumsum(hits, axis=0) - hits) * hits, axis=1)
    position = flat * capacity + rank
    source = (
        jnp.full((experts * capacity,), -1, dtype=jnp.int32)
        .at[position]
        .set(jnp.arange(tok_dev * top_k, dtype=jnp.int32))
    )
    live = source >= 0
    safe = jnp.maximum(source, 0)
    send_rows = jnp.where(live[:, None], hidden_a[safe // top_k], jnp.zeros((), jnp.bfloat16))
    send_rows = send_rows.reshape(experts, capacity, width)
    send_weights = jnp.where(live, gate_w.reshape(-1)[safe], jnp.zeros((), jnp.bfloat16))
    send_weights = send_weights.reshape(experts, capacity)
    weights = lax.all_to_all(
        send_weights, ("attn", "expert"), split_axis=0, concat_axis=0, tiled=True
    )
    senders, slots = weights.shape
    flat_rows = lax.all_to_all(
        send_rows, ("attn", "expert"), split_axis=0, concat_axis=0, tiled=True
    ).reshape(senders * slots, width)
    gate = jnp.dot(flat_rows, w_gate[0], preferred_element_type=jnp.float32)
    up = jnp.dot(flat_rows, w_up[0], preferred_element_type=jnp.float32)
    hidden = (jax.nn.silu(gate) * up).astype(jnp.bfloat16)
    down = jnp.dot(hidden, w_down[0], preferred_element_type=jnp.float32)
    scaled = weights.reshape(-1, 1).astype(jnp.float32) * down
    produced = scaled.astype(jnp.bfloat16).reshape(senders, slots, width)
    returned = lax.all_to_all(produced, ("attn", "expert"), split_axis=0, concat_axis=0, tiled=True)
    results = returned.reshape(experts * capacity, width)
    taken = results[position]
    return jnp.sum(taken.astype(jnp.float32).reshape(tok_dev, top_k, width), axis=1).astype(
        jnp.bfloat16
    )


def tiles_of(total, step):
    return [(at, min(step, total - at)) for at in range(0, total, step)]


def kernel(
    hidden_hbm, routes_hbm, gates_hbm, wg_hbm, wu_hbm, wd_hbm, out_ref,
    tokens, named, gates, wg, wu, wd, x, h, y, from_core, to_y, from_y, to_z, from_z,
    load_sem, ag_send, ag_recv, core_send, core_recv, y_send, y_recv, z_send, z_recv,
):
    top, rows = routes_hbm.shape
    width = hidden_hbm.shape[1]
    ff = wg_hbm.shape[2]
    quad = FAR * rows

    group = lax.axis_index("groups")
    core = lax.axis_index("attn")
    place = lax.axis_index("expert")
    far, near = place // 2, place % 2
    own = core * lax.axis_size("expert") + place

    fars = [far, far + 1 - 2 * (far % 2), (far + 2) % FAR, FAR - 1 - far]
    sibling = (group, 1 - core, place)
    beside = (group, core, far * 2 + 1 - near)
    along = [(group, core, f * 2 + near) for f in fars]

    inputs = [
        pltpu.make_async_copy(src, dst, load_sem.at[i])
        for i, (src, dst) in enumerate(((hidden_hbm, tokens), (routes_hbm, named), (gates_hbm, gates)))
    ]
    loads = [
        pltpu.make_async_copy(src.at[0], dst, load_sem.at[3 + i])
        for i, (src, dst) in enumerate(((wg_hbm, wg), (wu_hbm, wu), (wd_hbm, wd)))
    ]
    for load in inputs:
        load.start()

    barrier = pltpu.get_barrier_semaphore()
    partners = [sibling, beside] + along[1:]
    for partner in partners:
        pl.semaphore_signal(barrier, inc=1, device_id=partner, device_id_type=MESH)

    for load in loads:
        load.start()
    for load in inputs:
        load.wait()

    start = width // LANES * LANES
    rest = width - start
    x[0:rows, 0:start] = tokens[:, 0:start]
    lane = lax.broadcasted_iota(jnp.int32, (LANES, rows), 0)
    weights = gates[...].astype(jnp.float32)
    table = jnp.zeros((LANES, rows), jnp.float32)
    for k in range(top):
        table += jnp.where(lane == named[k : k + 1, :] + rest, weights[k : k + 1, :], 0.0)
    last = jnp.concatenate(
        [tokens[:, start:].astype(jnp.float32), jnp.zeros((rows, LANES - rest), jnp.float32)], axis=1
    )
    x[0:rows, start : start + LANES] = (table.T + last).astype(jnp.bfloat16)
    pl.semaphore_wait(barrier, len(partners))

    half = rows

    def piece(dy, dc, d, p):
        return x.at[pl.ds(((dy * 2 + dc) * FAR + d) * rows + p * half, half)]

    def remote(src, dst, send, recv, device):
        return pltpu.make_async_remote_copy(
            src_ref=src, dst_ref=dst, send_sem=send, recv_sem=recv,
            device_id=device, device_id_type=MESH,
        )

    def gather(src, dst, i, device):
        return remote(src, dst, ag_send.at[i], ag_recv.at[i], device)

    middle = (far + 1) // 2 == 1
    pieces = range(1)
    gather_z = {
        (d, p): gather(piece(0, 0, 0, p), piece(0, 0, d, p), (d - 1) * 2 + p, along[d])
        for d in (1, 2, 3) for p in pieces
    }
    gather_y = {
        (d, p): gather(piece(0, 0, d, p), piece(1, 0, d, p), 6 + d * 2 + p, beside)
        for d in range(FAR) for p in pieces
    }
    gather_c = {
        (dy, d, p): gather(piece(dy, 0, d, p), piece(dy, 1, d, p), 14 + (dy * FAR + d) * 2 + p, sibling)
        for dy in range(2) for d in range(FAR) for p in pieces
    }
    passed = {
        p: remote(piece(0, 0, 2, p), piece(0, 0, 3, p), ag_send.at[30 + p], ag_recv.at[4 + p], along[1])
        for p in pieces
    }
    for p in pieces:
        gather_z[2, p].start()
        gather_z[1, p].start()
        gather_y[0, p].start()

    @pl.when(middle)
    def _():
        for p in pieces:
            gather_z[3, p].start()

    for p in pieces:
        gather_c[0, 0, p].start()
    for d, p in ((1, 0), (2, 0), (3, 0)):
        gather_z[d, p].wait_recv()
        if d == 2:

            @pl.when(middle)
            def _():
                passed[p].start()

        gather_y[d, p].start()
        gather_c[0, d, p].start()

    n_ff = tiles_of(ff, 512)
    n_out = tiles_of(width, 256)
    scale = {}

    def up_tile(dy, at, size):
        block = x[dy * 2 * quad : (dy + 1) * 2 * quad, 0:width]
        gate = jnp.dot(block, wg[:, at : at + size], preferred_element_type=jnp.float32)
        up = jnp.dot(block, wu[:, at : at + size], preferred_element_type=jnp.float32)
        h[:, at : at + size] = (gate / (1.0 + jnp.exp(-gate)) * up).astype(jnp.bfloat16)

    def down_tile(dy, at, size):
        if dy not in scale:
            tail = x[dy * 2 * quad : (dy + 1) * 2 * quad, start : start + LANES].astype(jnp.float32)
            lanes = lax.broadcasted_iota(jnp.int32, tail.shape, 1)
            scale[dy] = jnp.sum(jnp.where(lanes == own + rest, tail, 0.0), axis=1, keepdims=True)
        down = jnp.dot(h[...], wd[:, at : at + size], preferred_element_type=jnp.float32)
        y[dy * 2 * quad : (dy + 1) * 2 * quad, at : at + size] = (scale[dy] * down).astype(jnp.bfloat16)

    early = remote(
        y.at[pl.ds(quad, quad)], from_core.at[pl.ds(0, quad)], core_send.at[0], core_recv.at[0], sibling
    )

    def core_copy(j):
        columns = pl.ds(*n_out[j])
        return remote(
            y.at[pl.ds(3 * quad, quad), columns],
            from_core.at[pl.ds(quad, quad), columns],
            core_send.at[1 + j], core_recv.at[1 + j], sibling,
        )

    def y_copy(j):
        columns = pl.ds(*n_out[j])
        return remote(to_y.at[:, columns], from_y.at[:, columns], y_send.at[j], y_recv.at[j], beside)

    def z_copy(j, d):
        columns = pl.ds(*n_out[j])
        i = j * 3 + d - 1
        return remote(
            to_z.at[pl.ds(d * rows, rows), columns], from_z.at[pl.ds(d * rows, rows), columns],
            z_send.at[i], z_recv.at[i], along[d],
        )

    for d in range(FAR):
        for p in pieces:
            gather_c[0, d, p].wait_recv()
    loads[0].wait()
    loads[1].wait()
    for at, size in n_ff:
        up_tile(0, at, size)
    queue = [(0, 0), (1, 0), (2, 0), (3, 0)]

    def hand_on(many):
        for _ in range(many):
            d, p = queue.pop(0)
            gather_y[d, p].wait_recv()
            gather_c[1, d, p].start()

    hand_on(2)
    loads[2].wait()
    for j, (at, size) in enumerate(n_out):
        down_tile(0, at, size)
        if j >= 1 and len(queue) > 0:
            hand_on(1)
    hand_on(len(queue))
    early.start()

    for d in range(FAR):
        for p in pieces:
            gather_c[1, d, p].wait_recv()
    for at, size in n_ff:
        up_tile(1, at, size)

    def after_core(j):
        at, size = n_out[j]
        core_copy(j).wait_recv()
        to_y[:, at : at + size] = (
            y[2 * quad : 3 * quad, at : at + size].astype(jnp.float32)
            + from_core[quad : 2 * quad, at : at + size].astype(jnp.float32)
        ).astype(jnp.bfloat16)
        y_copy(j).start()

    def after_y(j):
        at, size = n_out[j]
        y_copy(j).wait_recv()
        to_z[:, at : at + size] = (
            y[0:quad, at : at + size].astype(jnp.float32)
            + from_core[0:quad, at : at + size].astype(jnp.float32)
            + from_y[:, at : at + size].astype(jnp.float32)
        ).astype(jnp.bfloat16)
        for d in (3, 2, 1):
            z_copy(j, d).start()

    count = len(n_out)
    for j, (at, size) in enumerate(n_out):
        down_tile(1, at, size)
        core_copy(j).start()
        if j >= 1:
            after_core(j - 1)
    after_core(count - 1)
    early.wait_recv()
    for j in range(count):
        after_y(j)
    for j, (at, size) in enumerate(n_out):
        total = to_z[0:rows, at : at + size].astype(jnp.float32)
        for d in (1, 2, 3):
            z_copy(j, d).wait_recv()
            total += from_z[d * rows : (d + 1) * rows, at : at + size].astype(jnp.float32)
        out_ref[:, at : at + size] = total.astype(jnp.bfloat16)

    for d in (1, 2):
        for p in pieces:
            gather_z[d, p].wait_send()

    @pl.when(middle)
    def _():
        for p in pieces:
            gather_z[3, p].wait_send()
            passed[p].wait_send()

    for copy in [*gather_y.values(), *gather_c.values()]:
        copy.wait_send()
    early.wait_send()
    for j in range(count):
        core_copy(j).wait_send()
        y_copy(j).wait_send()
        for d in (1, 2, 3):
            z_copy(j, d).wait_send()


def gather_body(hidden_a, routes, gate_w, w_gate, w_up, w_down):
    experts = lax.axis_size(("attn", "expert"))
    rows, width = hidden_a.shape
    ff = w_gate.shape[2]
    wide = -(-width // LANES) * LANES
    quad = FAR * rows
    count = len(tiles_of(width, 256))
    vmem = pl.BlockSpec(memory_space=pltpu.VMEM)
    hbm = pl.BlockSpec(memory_space=pl.ANY)
    dma = pltpu.SemaphoreType.DMA
    tokens = experts * rows
    return pl.pallas_call(
        kernel,
        out_shape=jax.ShapeDtypeStruct((rows, width), jnp.bfloat16),
        in_specs=[hbm] * 6,
        out_specs=vmem,
        scratch_shapes=[
            pltpu.VMEM((rows, width), jnp.bfloat16),
            pltpu.VMEM(routes.shape[::-1], jnp.int32),
            pltpu.VMEM(gate_w.shape[::-1], jnp.bfloat16),
            pltpu.VMEM((width, ff), jnp.bfloat16),
            pltpu.VMEM((width, ff), jnp.bfloat16),
            pltpu.VMEM((ff, width), jnp.bfloat16),
            pltpu.VMEM((tokens, wide), jnp.bfloat16),
            pltpu.VMEM((tokens // 2, ff), jnp.bfloat16),
            pltpu.VMEM((tokens, width), jnp.bfloat16),
            pltpu.VMEM((tokens // 2, width), jnp.bfloat16),
            pltpu.VMEM((quad, width), jnp.bfloat16),
            pltpu.VMEM((quad, width), jnp.bfloat16),
            pltpu.VMEM((quad, width), jnp.bfloat16),
            pltpu.VMEM((quad, width), jnp.bfloat16),
            dma((6,)),
            dma((32,)),
            dma((30,)),
            dma((1 + count,)),
            dma((1 + count,)),
            dma((count,)),
            dma((count,)),
            dma((3 * count,)),
            dma((3 * count,)),
        ],
        compiler_params=pltpu.CompilerParams(
            collective_id=0, has_side_effects=True, vmem_limit_bytes=56 * 1024 * 1024
        ),
        cost_estimate=pl.CostEstimate(
            flops=6 * tokens * width * ff, bytes_accessed=6 * width * ff, transcendentals=tokens * ff
        ),
    )(hidden_a, routes.T, gate_w.T, w_gate, w_up, w_down)


def solution(mesh):
    placed = (
        P(("groups", "attn", "expert"), None),
        P(("groups", "attn", "expert"), None),
        P(("groups", "attn", "expert"), None),
        P(("attn", "expert"), None, None),
        P(("attn", "expert"), None, None),
        P(("attn", "expert"), None, None),
    )
    small = mesh.shape["attn"] == 2 and mesh.shape["expert"] == 2 * FAR
    return jax.shard_map(
        gather_body if small else exchange_body,
        mesh=mesh,
        in_specs=placed,
        out_specs=P(("groups", "attn", "expert"), None),
        check_vma=False,
    )
```
